256 devices in a mesh: bx: 64 (over x, z, core), bz: 4 (over y).
Axes of the slice: x: 4, y: 4, z: 8, core: 2. Of those that a mesh axis runs over, the one named last changes fastest.
Arguments:
- fields: float32 [3, 512, 256, 512], P(None, 'bx', None, 'bz'), may hold values from 0.2 to 2
- conductance: float32 [512, 256, 512], P('bx', None, 'bz'), may hold values from 0.25 to 1
- absorption: float32 [512, 256, 512], P('bx', None, 'bz'), may hold values from 0.0001 to 0.01
- occupancy: int32 [64, 16, 16], P('bx', None, 'bz'), may hold values 0 or 1
- facing: int32 [16, 16], P(None, 'bz'), may hold values 0 or 1
Outputs:
- advanced: float32 [3, 512, 256, 512], P(None, 'bx', None, 'bz')
- picture: float32 [4, 256, 512], P(None, 'bx', 'bz')
The draws below stay inside these ranges and needn't reach their ends.
All inputs are finite; a program needn't handle non-finite values. No bound on the sum of `occupancy` or of `facing` on one device may be relied on, other than what follows from the above.
Results may differ from the reference program's by a relative error of at most 0.00012.
Values sent between devices are 32-bit elements; how exact they have to be, the bound alone decides.
A program may use at most 128 MiB of HBM per device.

```python
import math
import jax
import jax.numpy as jnp

CX = 8
NY = 256
TY = 16
TZ = 32
NX = 512
NZ = 512
N_BX = 64


def set_ends(entries, stream_key, low, high):
    shape = entries.shape
    index_at = [jax.random.randint(jax.random.fold_in(stream_key, axis), (), 0, shape[axis]) for axis in range(len(shape))]
    entries = entries.at[tuple(index_at)].set(low)
    longest = shape.index(max(shape))
    index_at[longest] = (index_at[longest] + 1) % shape[longest]
    return entries.at[tuple(index_at)].set(high)


def levels(own_key, dims, cuts, least, high):
    factor_of, own = 1.0, jax.random.fold_in(own_key, 6)
    for axis_at, blocks in cuts:
        heights = jnp.exp(jax.random.uniform(jax.random.fold_in(own, axis_at), (blocks,), jnp.float32, least / len(cuts), high / len(cuts)))
        factor_of = factor_of * jnp.repeat(heights, dims[axis_at] // blocks).reshape([-1 if axis == axis_at else 1 for axis in range(len(dims))])
    return factor_of


def setup_inputs(seed: int = 0) -> dict:
    arg_keys = jax.random.split(jax.random.key(seed), 6)
    return {
        "fields": jnp.clip(0.2 + 1.8 * jax.random.uniform(arg_keys[0], (3, NX, NY, NZ), jnp.float32) ** levels(arg_keys[0], (3, NX, NY, NZ), ((1, 64), (3, 4)), -0.2, 0.2), 0.2, 2.0),
        "conductance": jnp.clip(0.25 + 0.75 * jax.random.uniform(arg_keys[1], (NX, NY, NZ), jnp.float32) ** levels(arg_keys[1], (NX, NY, NZ), ((0, 64), (2, 4)), -0.2, 0.2), 0.25, 1.0),
        "absorption": jnp.clip(jnp.exp(math.log(0.01) - 4.6051702 * jax.random.uniform(arg_keys[2], (NX, NY, NZ), jnp.float32) ** levels(arg_keys[2], (NX, NY, NZ), ((0, 64), (2, 4)), -0.2, 0.2)), 0.0001, 0.01),
        "occupancy": set_ends((jax.random.randint(arg_keys[3], (N_BX, NY // TY, NZ // TZ), 0, 4) < 3).astype(jnp.int32), jax.random.fold_in(arg_keys[3], 1), 0, 1),
        "facing": set_ends((jax.random.randint(arg_keys[4], (NY // TY, NZ // TZ), 0, 2) < 1).astype(jnp.int32), jax.random.fold_in(arg_keys[4], 1), 0, 1),
    }


def advance(padded):
    centre = padded[:, 1:-1, 1:-1, 1:-1]
    values = centre[:3]
    own = centre[3]
    neighbours = (padded[:, 2:, 1:-1, 1:-1], padded[:, :-2, 1:-1, 1:-1],
                  padded[:, 1:-1, 2:, 1:-1], padded[:, 1:-1, :-2, 1:-1],
                  padded[:, 1:-1, 1:-1, 2:], padded[:, 1:-1, 1:-1, :-2])
    change = jnp.zeros_like(values)
    for beside in neighbours:
        change = change + 0.5 * (own + beside[3]) * (beside[:3] - values)
    return values + change / 7.0


def march(advanced, extinction):
    running = jnp.cumsum(extinction, axis=0)
    total = running[-1]
    ahead = running - extinction
    behind = total[None] - running
    glow = advanced * (1.0 - jnp.exp(-extinction))[None]
    front = jnp.sum(glow * jnp.exp(-ahead)[None], axis=1)
    back = jnp.sum(glow * jnp.exp(-behind)[None], axis=1)
    return front, back, total


def tile_map(flags, rows_each, cols_each):
    height = flags.shape[0]
    width = flags.shape[1]
    spread = jnp.broadcast_to(flags[:, None, :, None], (height, rows_each, width, cols_each))
    return spread.reshape(height * rows_each, width * cols_each).astype(jnp.float32)


def reference(fields, conductance, absorption, occupancy, facing):
    stacked = jnp.concatenate([fields, conductance[None]], 0)
    padded = jnp.pad(stacked, ((0, 0), (1, 1), (1, 1), (1, 1)))
    advanced = advance(padded)
    cell_mask = jnp.repeat(jnp.repeat(jnp.repeat(occupancy, CX, axis=0), TY, axis=1), TZ, axis=2).astype(jnp.float32)
    extinction = absorption * advanced[0] * cell_mask
    front, back, total = march(advanced, extinction)
    flip = tile_map(facing, TY, TZ)
    colour = jnp.where(flip > 0.5, back, front)
    picture = jnp.concatenate([colour, (1.0 - jnp.exp(-total))[None]], 0)
    return advanced, picture
```

```python
import functools

import jax
import jax.numpy as jnp
from jax import lax
from jax.experimental import pallas as pl
from jax.experimental.pallas import tpu as pltpu
from jax.sharding import PartitionSpec as P

MESH = pl.DeviceIdType.MESH
TY = 16
TZ = 32
ZS = 8
PAD = 8


def tile_lanes(flag, row, lane):
    out = jnp.where(lane < TZ, flag(row, 0), flag(row, 1))
    out = jnp.where(lane < 2 * TZ, out, flag(row, 2))
    return jnp.where(lane < 3 * TZ, out, flag(row, 3)).astype(jnp.float32)


def kernel(
    n_bx, n_bz, cx, ny,
    fields, cond, absn, occ, facing,
    adv, pic,
    u, k, ab, lo_u, lo_k, hi_u, hi_k, zs, zl, zr, occ_m, fac_m, pair, give, ready, got,
    in_sem, hs_sem, hr_sem, zs_sem, zr_sem, cs_sem, cr_sem, as_sem, ar_sem,
):
    xs = n_bx // (2 * ZS)
    nb = xs
    rows = ny // nb
    groups = rows // 8
    bx = lax.axis_index("bx")
    bz = lax.axis_index("bz")
    core = bx % 2
    z = (bx // 2) % ZS
    x = bx // (2 * ZS)
    has_lo, has_hi = bx > 0, bx < n_bx - 1
    has_l, has_r = bz > 0, bz < n_bz - 1
    lo_id, hi_id = (bx - 1, bz), (bx + 1, bz)
    l_id, r_id = (bx, bz - 1), (bx, bz + 1)
    lo_x = (bx - 1) // (2 * ZS)
    hi_x = (bx + 1) // (2 * ZS)
    mate = (bx + 1 - 2 * core, bz)

    def start_row(of_x, b):
        return pl.multiple_of(((of_x + b) % nb) * rows, rows)

    def chip_id(dx, dz):
        return ((((x + dx) % xs) * ZS + (z + dz) % ZS) * 2 + core, bz)

    barrier = pltpu.get_barrier_semaphore()

    def greet(who):
        pl.semaphore_signal(barrier, inc=1, device_id=who, device_id_type=MESH)

    for dx in range(xs):
        for dz in range(ZS):
            if (dx, dz) != (0, 0):
                greet(chip_id(dx, dz))
    for cond_, who in ((has_lo, lo_id), (has_hi, hi_id), (has_l, l_id), (has_r, r_id)):
        @pl.when(cond_)
        def _():
            greet(who)

    def loads(b):
        at = pl.ds(start_row(x, b), rows)
        to = pl.ds(start_row(x, b) + PAD, rows)
        return (
            pltpu.make_async_copy(fields.at[:, :, at, :], u.at[:, :, to, :], in_sem.at[b, 0]),
            pltpu.make_async_copy(cond.at[:, at, :], k.at[:, to, :], in_sem.at[b, 1]),
            pltpu.make_async_copy(absn.at[:, at, :], ab.at[:, at, :], in_sem.at[b, 2]),
        )

    for b in range(nb):
        for c in loads(b):
            c.start()

    for p in range(cx):
        k[p, 0:PAD, :] = jnp.zeros((PAD, 128), jnp.float32)
        k[p, PAD + ny : 2 * PAD + ny, :] = jnp.zeros((PAD, 128), jnp.float32)
        for a in range(3):
            u[a, p, 0:PAD, :] = jnp.zeros((PAD, 128), jnp.float32)
            u[a, p, PAD + ny : 2 * PAD + ny, :] = jnp.zeros((PAD, 128), jnp.float32)

    @pl.when(bx == 0)
    def _():
        lo_u[...] = jnp.zeros_like(lo_u)
        lo_k[...] = jnp.zeros_like(lo_k)

    @pl.when(bx == n_bx - 1)
    def _():
        hi_u[...] = jnp.zeros_like(hi_u)
        hi_k[...] = jnp.zeros_like(hi_k)

    @pl.when(bz == 0)
    def _():
        zl[...] = jnp.zeros_like(zl)

    @pl.when(bz == n_bz - 1)
    def _():
        zr[...] = jnp.zeros_like(zr)

    lane = lax.broadcasted_iota(jnp.int32, (8, 128), 1)
    lane1 = lax.broadcasted_iota(jnp.int32, (1, 128), 1)
    for t in range(ny // TY):
        occ_m[t : t + 1, :] = tile_lanes(lambda i, j: occ[0, i, j], t, lane1)
        fac_m[t : t + 1, :] = tile_lanes(lambda i, j: facing[i, j], t, lane1)

    pl.semaphore_wait(
        barrier,
        xs * ZS - 1 + has_lo.astype(jnp.int32) + has_hi.astype(jnp.int32)
        + has_l.astype(jnp.int32) + has_r.astype(jnp.int32),
    )

    def halo(b, up):
        of_x, who, p = (hi_x, hi_id, cx - 1) if up else (lo_x, lo_id, 0)
        to_u, to_k = (lo_u, lo_k) if up else (hi_u, hi_k)
        at = pl.ds(start_row(of_x, b), rows)
        d = int(up)
        return (
            pltpu.make_async_remote_copy(
                fields.at[:, p, at, :], to_u.at[:, at, :], hs_sem.at[b, d, 0], hr_sem.at[b, d, 0],
                device_id=who, device_id_type=MESH),
            pltpu.make_async_remote_copy(
                cond.at[p, at, :], to_k.at[at, :], hs_sem.at[b, d, 1], hr_sem.at[b, d, 1],
                device_id=who, device_id_type=MESH),
        )

    for b in range(nb):
        @pl.when(has_lo)
        def _():
            for c in halo(b, False):
                c.start()

        @pl.when(has_hi)
        def _():
            for c in halo(b, True):
                c.start()

    slot = ((lane + 1) % 128) // 2

    def edge(b, right):
        return pltpu.make_async_remote_copy(
            zs.at[b], (zl if right else zr).at[b], zs_sem.at[b, int(right)], zr_sem.at[b, int(right)],
            device_id=r_id if right else l_id, device_id_type=MESH)

    def pack_batch(b, carry):
        for c in loads(b):
            c.wait()
        r0 = start_row(x, b)

        def pack(g, carry):
            at = pl.ds(pl.multiple_of(r0 + g * 8, 8) + PAD, 8)
            out = jnp.zeros((8, 128), jnp.float32)
            for p in range(cx):
                for a in range(4):
                    j = p * 4 + a
                    v = k[p, at, :] if a == 3 else u[a, p, at, :]
                    if j:
                        v = pltpu.roll(v, 2 * j, 1)
                    out = jnp.where(slot == j, v, out)
            zs[b, pl.ds(pl.multiple_of(g * 8, 8), 8), :] = out
            return carry

        lax.fori_loop(0, groups, pack, 0)

        @pl.when(has_l)
        def _():
            edge(b, False).start()

        @pl.when(has_r)
        def _():
            edge(b, True).start()

        return carry

    lax.fori_loop(0, nb, pack_batch, 0)

    def core_copy(b):
        return pltpu.make_async_remote_copy(
            give.at[b], pair.at[b, core], cs_sem.at[b], cr_sem.at[b], device_id=mate, device_id_type=MESH)

    def send_out(b, e):
        far = 4 + ((e + 1) // 2) * (2 * (e % 2) - 1)
        dest = (z + far) % ZS
        return dest, pltpu.make_async_remote_copy(
            ready.at[b, dest], got.at[x * ZS + z], as_sem.at[b, e], ar_sem.at[x * ZS + z],
            device_id=chip_id(b, far), device_id_type=MESH)

    def wait_halo(b):
        @pl.when(has_lo)
        def _():
            for c in halo(b, True):
                c.wait_recv()

        @pl.when(has_hi)
        def _():
            for c in halo(b, False):
                c.wait_recv()

        @pl.when(has_l)
        def _():
            edge(b, True).wait_recv()

        @pl.when(has_r)
        def _():
            edge(b, False).wait_recv()

    def work(b):
        wait_halo(b)
        r0 = start_row(x, b)

        def step(g, carry):
            y0 = pl.multiple_of(r0 + g * 8, 8)
            at = pl.ds(y0, 8)
            mid = pl.ds(y0 + PAD, 8)
            above = pl.ds(y0 + PAD + 1, 8)
            below = pl.ds(y0 + PAD - 1, 8)
            here = pl.ds(pl.multiple_of(g * 8, 8), 8)
            edges = jnp.where(lane % 2 == 0, zr[b, here, :], pltpu.roll(zl[b, here, :], 2, 1))
            tile = y0 // TY
            mask = occ_m[pl.ds(tile, 1), :]
            flip = jnp.broadcast_to(fac_m[pl.ds(tile, 1), :] > 0.5, (8, 128))
            first, last = lane == 0, lane == 127

            k_prev = lo_k[at, :]
            u_prev = [lo_u[a, at, :] for a in range(3)]
            k_here = k[0, mid, :]
            u_here = [u[a, 0, mid, :] for a in range(3)]
            flow = [(k_prev + k_here) * (u_prev[a] - u_here[a]) for a in range(3)]
            through = jnp.ones((8, 128), jnp.float32)
            colour = [jnp.zeros((8, 128), jnp.float32)] * 3
            for p in range(cx):
                if p < cx - 1:
                    k_next = k[p + 1, mid, :]
                    u_next = [u[a, p + 1, mid, :] for a in range(3)]
                else:
                    k_next = hi_k[at, :]
                    u_next = [hi_u[a, at, :] for a in range(3)]
                k_x = k_here + k_next
                k_a = k_here + k[p, above, :]
                k_b = k_here + k[p, below, :]
                e = pltpu.roll(edges, 127 - 2 * (p * 4 + 3), 1)
                k_l = k_here + jnp.where(first, e, pltpu.roll(k_here, 1, 1))
                k_r = k_here + jnp.where(last, e, pltpu.roll(k_here, 127, 1))
                new = []
                for a in range(3):
                    v = u_here[a]
                    next_flow = k_x * (u_next[a] - v)
                    change = flow[a] + next_flow
                    change = change + k_a * (u[a, p, above, :] - v)
                    change = change + k_b * (u[a, p, below, :] - v)
                    e = pltpu.roll(edges, 127 - 2 * (p * 4 + a), 1)
                    change = change + k_l * (jnp.where(first, e, pltpu.roll(v, 1, 1)) - v)
                    change = change + k_r * (jnp.where(last, e, pltpu.roll(v, 127, 1)) - v)
                    flow[a] = -next_flow
                    out = v + change * (0.5 / 7.0)
                    adv[a, p, at, :] = out
                    new.append(out)
                extinction = ab[p, at, :] * new[0] * mask
                passed = jnp.exp(-extinction)
                glow = (1.0 - passed) * jnp.where(flip, 1.0, through)
                keep = jnp.where(flip, passed, 1.0)
                colour = [colour[a] * keep + new[a] * glow for a in range(3)]
                through = through * passed
                k_here, u_here = k_next, u_next
            for c, v in enumerate(colour + [through]):
                top, bottom = v[0:4], v[4:8]
                pair[b, core, g, c] = jnp.where(core == 0, top, bottom)
                give[b, g, c] = jnp.where(core == 0, bottom, top)
            return carry

        lax.fori_loop(0, groups, step, 0)
        core_copy(b).start()

    def merge(b):
        core_copy(b).wait_recv()
        tile0 = (start_row(x, b) // TY)

        def step(g, carry):
            flip = jnp.broadcast_to(fac_m[pl.ds(tile0 + g // 2, 1), :] > 0.5, (4, 128))
            t0, t1 = pair[b, 0, g, 3], pair[b, 1, g, 3]
            for c in range(3):
                c0, c1 = pair[b, 0, g, c], pair[b, 1, g, c]
                ready[b, g, c] = jnp.where(flip, c1 + t1 * c0, c0 + t0 * c1)
            ready[b, g, 3] = t0 * t1
            return carry

        lax.fori_loop(0, groups, step, 0)
        for e in range(ZS):
            _, c = send_out(b, e)
            if e < ZS - 1:
                c.start()
            else:
                @pl.when(b > 0)
                def _():
                    c.start()

    def batch(b, carry):
        @pl.when(b < nb)
        def _():
            work(b)

        @pl.when(b > 0)
        def _():
            merge(b - 1)

        return carry

    lax.fori_loop(0, nb + 1, batch, 0)

    flip = jnp.broadcast_to(fac_m[pl.ds(bx * 4 // TY, 1), :] > 0.5, (4, 128))
    me = x * ZS + z
    got[pl.ds(me, 1)] = ready[0, pl.ds(z, 1)]

    def gather(s, carry):
        colour, through = carry[:3], carry[3]

        @pl.when(s != me)
        def _():
            pltpu.make_async_remote_copy(
                ready.at[0, 0], got.at[s], as_sem.at[0, 0], ar_sem.at[s],
                device_id=mate, device_id_type=MESH).wait_recv()

        t = got[s, 3]
        colour = [
            jnp.where(flip, got[s, c] + t * colour[c], colour[c] + through * got[s, c]) for c in range(3)
        ]
        return (*colour, through * t)

    zero = jnp.zeros((4, 128), jnp.float32)
    out = lax.fori_loop(0, xs * ZS, gather, (zero, zero, zero, jnp.ones((4, 128), jnp.float32)))
    for c in range(3):
        pic[c] = out[c]
    pic[3] = 1.0 - out[3]

    def drain(b, carry):
        @pl.when(has_lo)
        def _():
            for c in halo(b, False):
                c.wait_send()

        @pl.when(has_hi)
        def _():
            for c in halo(b, True):
                c.wait_send()

        @pl.when(has_l)
        def _():
            edge(b, False).wait_send()

        @pl.when(has_r)
        def _():
            edge(b, True).wait_send()

        core_copy(b).wait_send()
        for e in range(ZS):
            _, c = send_out(b, e)
            if e < ZS - 1:
                c.wait_send()
            else:
                @pl.when(b > 0)
                def _():
                    c.wait_send()
        return carry

    lax.fori_loop(0, nb, drain, 0)


def solution(mesh):
    n_bx, n_bz = mesh.shape["bx"], mesh.shape["bz"]

    def shards(fields, conductance, absorption, occupancy, facing):
        _, cx, ny, nz = fields.shape
        xs = n_bx // (2 * ZS)
        nb, rows = xs, ny // xs
        f32 = jnp.float32
        vmem, dma = pltpu.VMEM, pltpu.SemaphoreType.DMA
        hbm = pl.BlockSpec(memory_space=pl.ANY)
        smem = pl.BlockSpec(memory_space=pltpu.SMEM)
        in_vmem = pl.BlockSpec(memory_space=pltpu.VMEM)
        return pl.pallas_call(
            functools.partial(kernel, n_bx, n_bz, cx, ny),
            out_shape=(
                jax.ShapeDtypeStruct(fields.shape, f32),
                jax.ShapeDtypeStruct((4, ny // n_bx, nz), f32),
            ),
            in_specs=[hbm, hbm, hbm, smem, smem],
            out_specs=(in_vmem, in_vmem),
            scratch_shapes=[
                vmem((3, cx, ny + 2 * PAD, nz), f32),
                vmem((cx, ny + 2 * PAD, nz), f32),
                vmem((cx, ny, nz), f32),
                vmem((3, ny, nz), f32),
                vmem((ny, nz), f32),
                vmem((3, ny, nz), f32),
                vmem((ny, nz), f32),
                vmem((nb, rows, nz), f32),
                vmem((nb, rows, nz), f32),
                vmem((nb, rows, nz), f32),
                vmem((ny // TY, nz), f32),
                vmem((ny // TY, nz), f32),
                vmem((nb, 2, rows // 8, 4, 4, nz), f32),
                vmem((nb, rows // 8, 4, 4, nz), f32),
                vmem((nb, rows // 8, 4, 4, nz), f32),
                vmem((xs * ZS, 4, 4, nz), f32),
                dma((nb, 3)),
                dma((nb, 2, 2)),
                dma((nb, 2, 2)),
                dma((nb, 2)),
                dma((nb, 2)),
                dma((nb,)),
                dma((nb,)),
                dma((nb, ZS)),
                dma((xs * ZS,)),
            ],
            compiler_params=pltpu.CompilerParams(
                collective_id=0, has_side_effects=True, vmem_limit_bytes=30 << 20
            ),
            name="step_and_render",
        )(fields, conductance, absorption, occupancy, facing)

    return jax.shard_map(
        shards,
        mesh=mesh,
        in_specs=(
            P(None, "bx", None, "bz"),
            P("bx", None, "bz"),
            P("bx", None, "bz"),
            P("bx", None, "bz"),
            P(None, "bz"),
        ),
        out_specs=(P(None, "bx", None, "bz"), P(None, "bx", "bz")),
        check_vma=False,
    )
```

```python
import functools

import jax
import jax.numpy as jnp
from jax import lax
from jax.experimental import pallas as pl
from jax.experimental.pallas import tpu as pltpu
from jax.sharding import PartitionSpec as P

MESH = pl.DeviceIdType.MESH
TY = 16
TZ = 32
ZS = 8
PAD = 8
LIMIT = 30 << 20
SHARE = 0.5 / 7.0
PU, AU, BU = 2, 2, 2
EARLY = 2
NB = 4


def spread(flags):
    column = lax.broadcasted_iota(jnp.int32, (flags.shape[0], 128), 0)
    lane = lax.broadcasted_iota(jnp.int32, (flags.shape[0], 128), 1)
    own = (lane // TZ == column).astype(jnp.float32)
    return lax.dot_general(
        flags.astype(jnp.float32), own, (((0,), (0,)), ((), ())), preferred_element_type=jnp.float32
    )


def kernel(
    n_bx, n_bz, cx, ny,
    fields, cond, absn, occ, facing,
    adv, pic,
    u, k, ab, lo_u, lo_k, hi_u, hi_k, zs, zl, zr, occ_m, fac_m, pair, give, ready, got, flags,
    word, flag_sem, in_sem, hs_sem, hr_sem, zs_sem, zr_sem, cs_sem, cr_sem, as_sem, ar_sem,
):
    xs = n_bx // (2 * ZS)
    nb = NB
    m = xs // nb
    rows = ny // nb
    groups = rows // 8
    bx = lax.axis_index("bx")
    bz = lax.axis_index("bz")
    core = bx % 2
    z = (bx // 2) % ZS
    x = bx // (2 * ZS)
    has_lo, has_hi = bx > 0, bx < n_bx - 1
    has_l, has_r = bz > 0, bz < n_bz - 1
    lo_id, hi_id = (bx - 1, bz), (bx + 1, bz)
    l_id, r_id = (bx, bz - 1), (bx, bz + 1)
    lo_x = (bx - 1) // (2 * ZS)
    hi_x = (bx + 1) // (2 * ZS)
    mate = (bx + 1 - 2 * core, bz)

    def start_row(of_x, b):
        return pl.multiple_of(((of_x // m + b) % nb) * rows, rows)

    def chip_id(dx, dz):
        return ((((x + dx) % xs) * ZS + (z + dz) % ZS) * 2 + core, bz)

    barrier = pltpu.get_barrier_semaphore()
    line = [(0, dz) for dz in (1, ZS - 1, 2, ZS - 2, 3, ZS - 3, 4)] + [(dx, 0) for dx in range(1, xs)]

    def greet(sem, who):
        pl.semaphore_signal(sem, inc=1, device_id=who, device_id_type=MESH)

    for near, who in ((has_lo, lo_id), (has_hi, hi_id), (has_l, l_id), (has_r, r_id)):
        @pl.when(near)
        def _():
            greet(barrier, who)
    for dx, dz in line:
        greet(barrier, chip_id(dx, dz))

    def loads(b):
        at = pl.ds(start_row(x, b), rows)
        to = pl.ds(start_row(x, b) + PAD, rows)
        return (
            pltpu.make_async_copy(fields.at[:, :, at, :], u.at[:, :, to, :], in_sem.at[b, 0]),
            pltpu.make_async_copy(cond.at[:, at, :], k.at[:, to, :], in_sem.at[b, 1]),
            pltpu.make_async_copy(absn.at[:, at, :], ab.at[:, at, :], in_sem.at[b, 2]),
        )

    for b in range(nb):
        for c in loads(b)[:2]:
            c.start()
    for b in range(nb):
        loads(b)[2].start()

    lane = lax.broadcasted_iota(jnp.int32, (flags.shape[0], 128), 1)
    own = (lane // TZ == column).astype(jnp.float32)
    return lax.dot_general(
        flags.astype(jnp.float32), own, (((0,), (0,)), ((), ())), preferred_element_type=jnp.float32
    )


def kernel(
    n_bx, n_bz, cx, ny,
    fields, cond, absn, occ, facing,
    adv, pic,
    u, k, ab, lo_u, lo_k, hi_u, hi_k, zs, zl, zr, occ_m, fac_m, pair, give, ready, got, flags,
    word, flag_sem, in_sem, hs_sem, hr_sem, zs_sem, zr_sem, cs_sem, cr_sem, as_sem, ar_sem,
):
    xs = n_bx // (2 * ZS)
    nb = NB
    m = xs // nb
    rows = ny // nb
    groups = rows // 8
    bx = lax.axis_index("bx")
    bz = lax.axis_index("bz")
    core = bx % 2
    z = (bx // 2) % ZS
    x = bx // (2 * ZS)
    has_lo, has_hi = bx > 0, bx < n_bx - 1
    has_l, has_r = bz > 0, bz < n_bz - 1
    lo_id, hi_id = (bx - 1, bz), (bx + 1, bz)
    l_id, r_id = (bx, bz - 1), (bx, bz + 1)
    lo_x = (bx - 1) // (2 * ZS)
    hi_x = (bx + 1) // (2 * ZS)
    mate = (bx + 1 - 2 * core, bz)

    def start_row(of_x, b):
        return pl.multiple_of(((of_x // m + b) % nb) * rows, rows)

    def chip_id(dx, dz):
        return ((((x + dx) % xs) * ZS + (z + dz) % ZS) * 2 + core, bz)

    barrier = pltpu.get_barrier_semaphore()
    line = [(0, dz) for dz in (1, ZS - 1, 2, ZS - 2, 3, ZS - 3, 4)] + [(dx, 0) for dx in range(1, xs)]

    def greet(sem, who):
        pl.semaphore_signal(sem, inc=1, device_id=who, device_id_type=MESH)

    for near, who in ((has_lo, lo_id), (has_hi, hi_id), (has_l, l_id), (has_r, r_id)):
        @pl.when(near)
        def _():
            greet(barrier, who)
    for dx, dz in line:
        greet(barrier, chip_id(dx, dz))

    def loads(b):
        at = pl.ds(start_row(x, b), rows)
        to = pl.ds(start_row(x, b) + PAD, rows)
        return (
            pltpu.make_async_copy(fields.at[:, :, at, :], u.at[:, :, to, :], in_sem.at[b, 0]),
            pltpu.make_async_copy(cond.at[:, at, :], k.at[:, to, :], in_sem.at[b, 1]),
            pltpu.make_async_copy(absn.at[:, at, :], ab.at[:, at, :], in_sem.at[b, 2]),
        )

    for b in range(nb):
        for c in loads(b)[:2]:
            c.start()
    for b in range(nb):
        loads(b)[2].start()

    for p in range(cx):
        k[p, 0:PAD, :] = jnp.zeros((PAD, 128), jnp.float32)
        k[p, PAD + ny : 2 * PAD + ny, :] = jnp.zeros((PAD, 128), jnp.float32)
        for a in range(3):
            u[a, p, 0:PAD, :] = jnp.zeros((PAD, 128), jnp.float32)
            u[a, p, PAD + ny : 2 * PAD + ny, :] = jnp.zeros((PAD, 128), jnp.float32)

    @pl.when(bx == 0)
    def _():
        lo_u[...] = jnp.zeros_like(lo_u)
        lo_k[...] = jnp.zeros_like(lo_k)

    @pl.when(bx == n_bx - 1)
    def _():
        hi_u[...] = jnp.zeros_like(hi_u)
        hi_k[...] = jnp.zeros_like(hi_k)

    @pl.when(bz == 0)
    def _():
        zl[...] = jnp.zeros_like(zl)

    @pl.when(bz == n_bz - 1)
    def _():
        zr[...] = jnp.zeros_like(zr)

    lane = lax.broadcasted_iota(jnp.int32, (8, 128), 1)
    slot = ((lane + 1) % 128) // 2

    def edge(b, right):
        return pltpu.make_async_remote_copy(
            zs.at[b], (zl if right else zr).at[b], zs_sem.at[b, int(right)], zr_sem.at[b, int(right)],
            device_id=r_id if right else l_id, device_id_type=MESH)

    def pack_batch(b):
        for c in loads(b)[:2]:
            c.wait()
        r0 = start_row(x, b)

        def pack(g, carry):
            for h in range(PU):
                row = pl.multiple_of(g * (8 * PU), 8) + h * 8
                at = pl.ds(r0 + row + PAD, 8)
                parts = []
                for a in range(3):
                    out = jnp.zeros((8, 128), jnp.float32)
                    for p in range(cx):
                        j = 3 * p + a
                        v = u[a, p, at, :]
                        out = jnp.where(slot == j, pltpu.roll(v, 2 * j, 1) if j else v, out)
                    parts.append(out)
                out = jnp.zeros((8, 128), jnp.float32)
                for p in range(cx):
                    out = jnp.where(slot == 32 + 3 * p, pltpu.roll(k[p, at, :], 64 + 6 * p, 1), out)
                out = out + pltpu.roll(out, 2, 1) + pltpu.roll(out, 4, 1)
                zs[b, pl.ds(row, 8), :] = (parts[0] + parts[1]) + (parts[2] + out)
            return carry

        lax.fori_loop(0, groups // PU, pack, 0)

    def send_edges(b):
        @pl.when(has_l)
        def _():
            edge(b, False).start()

        @pl.when(has_r)
        def _():
            edge(b, True).start()

    first, last = lane == 0, lane == 127
    rim = first | last
    for b in range(min(EARLY, nb)):
        pack_batch(b)

    pl.semaphore_wait(
        barrier,
        len(line) + has_lo.astype(jnp.int32) + has_hi.astype(jnp.int32)
        + has_l.astype(jnp.int32) + has_r.astype(jnp.int32),
    )

    def halo(b, up):
        of_x, who, p = (hi_x, hi_id, cx - 1) if up else (lo_x, lo_id, 0)
        to_u, to_k = (lo_u, lo_k) if up else (hi_u, hi_k)
        at = pl.ds(start_row(of_x, b), rows)
        d = int(up)
        return (
            pltpu.make_async_remote_copy(
                fields.at[:, p, at, :], to_u.at[:, at, :], hs_sem.at[b, d, 0], hr_sem.at[b, d, 0],
                device_id=who, device_id_type=MESH),
            pltpu.make_async_remote_copy(
                cond.at[p, at, :], to_k.at[at, :], hs_sem.at[b, d, 1], hr_sem.at[b, d, 1],
                device_id=who, device_id_type=MESH),
        )

    for b in range(nb):
        @pl.when(has_lo)
        def _():
            for c in halo(b, False):
                c.start()

        @pl.when(has_hi)
        def _():
            for c in halo(b, True):
                c.start()

    for b in range(min(EARLY, nb)):
        send_edges(b)

    for dx, dz in line:
        greet(word, chip_id(dx, dz))

    flag_loads = [
        pltpu.make_async_copy(ref, flags.at[i], flag_sem.at[i]) for i, ref in enumerate((occ, facing))
    ]
    for c in flag_loads:
        c.start()

    def pack_rest(b, carry):
        pack_batch(b)
        send_edges(b)
        return carry

    if EARLY < nb:
        lax.fori_loop(EARLY, nb, pack_rest, 0)

    for c in flag_loads:
        c.wait()
    occ_m[...] = spread(flags[0])
    fac_m[...] = spread(flags[1])

    def interior(i, carry):
        for h in range(AU):
            y0 = pl.multiple_of(i * (8 * AU), 8) + h * 8
            at = pl.ds(y0, 8)
            mid = pl.ds(y0 + PAD, 8)
            above = pl.ds(y0 + PAD + 1, 8)
            below = pl.ds(y0 + PAD - 1, 8)
            k_here = k[0, mid, :]
            u_here = [u[a, 0, mid, :] for a in range(3)]
            flow = [None] * 3
            for p in range(cx):
                k_a = k_here + k[p, above, :]
                k_b = k_here + k[p, below, :]
                k_r = jnp.where(last, 0.0, k_here + pltpu.roll(k_here, 127, 1))
                if p < cx - 1:
                    k_next = k[p + 1, mid, :]
                    u_next = [u[a, p + 1, mid, :] for a in range(3)]
                    k_x = k_here + k_next
                for a in range(3):
                    v = u_here[a]
                    across = k_r * (pltpu.roll(v, 127, 1) - v)
                    change = across - pltpu.roll(across, 1, 1)
                    change = change + k_a * (u[a, p, above, :] - v)
                    change = change + k_b * (u[a, p, below, :] - v)
                    if p > 0:
                        change = change - flow[a]
                    if p < cx - 1:
                        flow[a] = k_x * (u_next[a] - v)
                        change = change + flow[a]
                    adv[a, p, at, :] = v + change * SHARE
                k_here, u_here = k_next, u_next
        return carry

    lax.fori_loop(0, ny // (8 * AU), interior, 0)
    for b in range(nb):
        loads(b)[2].wait()

    def core_copy(b):
        return pltpu.make_async_remote_copy(
            give.at[b], pair.at[b, core], cs_sem.at[b], cr_sem.at[b], device_id=mate, device_id_type=MESH)

    def send_out(b, i, e):
        far = 4 + ((e + 1) // 2) * (2 * (e % 2) - 1)
        to_x, to_z = ((x // m + b) % nb) * m + i, (z + far) % ZS
        return to_x, pltpu.make_async_remote_copy(
            ready.at[b, i * ZS + to_z], got.at[x * ZS + z], as_sem.at[b, i * ZS + e], ar_sem.at[x * ZS + z],
            device_id=((to_x * ZS + to_z) * 2 + core, bz), device_id_type=MESH)

    def each_out(b, act):
        for e in range(ZS):
            for i in range(m):
                to_x, c = send_out(b, i, e)
                if e < ZS - 1:
                    act(c)
                else:
                    @pl.when(to_x != x)
                    def _():
                        act(c)

    def wait_halo(b):
        @pl.when(has_lo)
        def _():
            for c in halo(b, True):
                c.wait_recv()

        @pl.when(has_hi)
        def _():
            for c in halo(b, False):
                c.wait_recv()

        @pl.when(has_l)
        def _():
            edge(b, True).wait_recv()

        @pl.when(has_r)
        def _():
            edge(b, False).wait_recv()

    def work(b):
        wait_halo(b)
        r0 = start_row(x, b)

        def step(i, carry):
            for h in range(BU):
                row = pl.multiple_of(i * (8 * BU), 8) + h * 8
                g = i * BU + h
                y0 = r0 + row
                at = pl.ds(y0, 8)
                mid = pl.ds(y0 + PAD, 8)
                here = pl.ds(row, 8)
                own = zs[b, here, :]
                other = jnp.where(lane % 2 == 1, pltpu.roll(zr[b, here, :], 127, 1), pltpu.roll(zl[b, here, :], 1, 1))
                into = pltpu.roll(own + other, 64, 1) * (other - own) * SHARE
                tile = y0 // TY
                mask = occ_m[pl.ds(tile, 1), :]
                flip = jnp.broadcast_to(fac_m[pl.ds(tile, 1), :] > 0.5, (8, 128))
                through = jnp.ones((8, 128), jnp.float32)
                colour = [jnp.zeros((8, 128), jnp.float32)] * 3
                for p in range(cx):
                    new = []
                    if p == 0:
                        k_x = (k[0, mid, :] + lo_k[at, :]) * SHARE
                    if p == cx - 1:
                        k_x = (k[p, mid, :] + hi_k[at, :]) * SHARE
                    for a in range(3):
                        j = 3 * p + a
                        out = adv[a, p, at, :]
                        out = out + jnp.where(rim, pltpu.roll(into, 128 - 2 * j, 1) if j else into, 0.0)
                        if p == 0:
                            out = out + k_x * (lo_u[a, at, :] - u[a, p, mid, :])
                        if p == cx - 1:
                            out = out + k_x * (hi_u[a, at, :] - u[a, p, mid, :])
                        adv[a, p, at, :] = out
                        new.append(out)
                    passed = jnp.exp(-(ab[p, at, :] * new[0] * mask))
                    glow = (1.0 - passed) * jnp.where(flip, 1.0, through)
                    keep = jnp.where(flip, passed, 1.0)
                    colour = [colour[a] * keep + new[a] * glow for a in range(3)]
                    through = through * passed
                for c, v in enumerate(colour + [through]):
                    top, bottom = v[0:4], v[4:8]
                    pair[b, core, g, c] = jnp.where(core == 0, top, bottom)
                    give[b, g, c] = jnp.where(core == 0, bottom, top)
            return carry

        lax.fori_loop(0, groups // BU, step, 0)
        core_copy(b).start()

    def merge(b):
        core_copy(b).wait_recv()
        tile0 = (start_row(x, b) // TY)

        def step(g, carry):
            flip = jnp.broadcast_to(fac_m[pl.ds(tile0 + g // 2, 1), :] > 0.5, (4, 128))
            t0, t1 = pair[b, 0, g, 3], pair[b, 1, g, 3]
            for c in range(3):
                c0, c1 = pair[b, 0, g, c], pair[b, 1, g, c]
                ready[b, g, c] = jnp.where(flip, c1 + t1 * c0, c0 + t0 * c1)
            ready[b, g, 3] = t0 * t1
            return carry

        lax.fori_loop(0, groups, step, 0)
        @pl.when(b == 0)
        def _():
            pl.semaphore_wait(word, len(line))

        each_out(b, lambda c: c.start())

    def batch(b, carry):
        @pl.when(b < nb)
        def _():
            work(b)

        @pl.when(b > 0)
        def _():
            merge(b - 1)

        return carry

    lax.fori_loop(0, nb + 1, batch, 0)

    def drain(b, carry):
        @pl.when(has_lo)
        def _():
            for c in halo(b, False):
                c.wait_send()

        @pl.when(has_hi)
        def _():
            for c in halo(b, True):
                c.wait_send()

        @pl.when(has_l)
        def _():
            edge(b, False).wait_send()

        @pl.when(has_r)
        def _():
            edge(b, True).wait_send()

        core_copy(b).wait_send()
        each_out(b, lambda c: c.wait_send())
        return carry

    lax.fori_loop(0, nb, drain, 0)

    flip = jnp.broadcast_to(fac_m[pl.ds(bx * 4 // TY, 1), :] > 0.5, (4, 128))
    me = x * ZS + z
    got[pl.ds(me, 1)] = ready[0, pl.ds(x % m * ZS + z, 1)]

    def gather(s, carry):
        colour, through = carry[:3], carry[3]

        @pl.when(s != me)
        def _():
            pltpu.make_async_remote_copy(
                ready.at[0, 0], got.at[s], as_sem.at[0, 0], ar_sem.at[s],
                device_id=mate, device_id_type=MESH).wait_recv()

        t = got[s, 3]
        colour = [
            jnp.where(flip, got[s, c] + t * colour[c], colour[c] + through * got[s, c]) for c in range(3)
        ]
        return (*colour, through * t)

    zero = jnp.zeros((4, 128), jnp.float32)
    out = lax.fori_loop(0, xs * ZS, gather, (zero, zero, zero, jnp.ones((4, 128), jnp.float32)))
    for c in range(3):
        pic[c] = out[c]
    pic[3] = 1.0 - out[3]


def hand_over(adv, pic, adv_out, pic_out, sem):
    cx = adv.shape[1]
    copies = [pltpu.make_async_copy(adv.at[:, p], adv_out.at[:, p], sem.at[p]) for p in range(cx)]
    copies.append(pltpu.make_async_copy(pic, pic_out, sem.at[cx]))
    for c in copies:
        c.start()
    for c in copies:
        c.wait()


def solution(mesh):
    n_bx, n_bz = mesh.shape["bx"], mesh.shape["bz"]

    def shards(fields, conductance, absorption, occupancy, facing):
        _, cx, ny, nz = fields.shape
        occupancy = occupancy[0].T
        facing = facing.T
        xs = n_bx // (2 * ZS)
        nb, rows = NB, ny // NB
        f32 = jnp.float32
        vmem, dma = pltpu.VMEM, pltpu.SemaphoreType.DMA
        hbm = pl.BlockSpec(memory_space=pltpu.HBM)
        in_vmem = pl.BlockSpec(memory_space=pltpu.VMEM)
        held = pl.pallas_call(
            functools.partial(kernel, n_bx, n_bz, cx, ny),
            out_shape=(
                jax.ShapeDtypeStruct(fields.shape, f32),
                jax.ShapeDtypeStruct((4, ny // n_bx, nz), f32),
            ),
            in_specs=[hbm] * 5,
            out_specs=(in_vmem, in_vmem),
            scratch_shapes=[
                vmem((3, cx, ny + 2 * PAD, nz), f32),
                vmem((cx, ny + 2 * PAD, nz), f32),
                vmem((cx, ny, nz), f32),
                vmem((3, ny, nz), f32),
                vmem((ny, nz), f32),
                vmem((3, ny, nz), f32),
                vmem((ny, nz), f32),
                vmem((nb, rows, nz), f32),
                vmem((nb, rows, nz), f32),
                vmem((nb, rows, nz), f32),
                vmem((ny // TY, nz), f32),
                vmem((ny // TY, nz), f32),
                vmem((nb, 2, rows // 8, 4, 4, nz), f32),
                vmem((nb, rows // 8, 4, 4, nz), f32),
                vmem((nb, rows // 8, 4, 4, nz), f32),
                vmem((xs * ZS, 4, 4, nz), f32),
                vmem((2,) + facing.shape, jnp.int32),
                pltpu.SemaphoreType.REGULAR,
                dma((2,)),
                dma((nb, 3)),
                dma((nb, 2, 2)),
                dma((nb, 2, 2)),
                dma((nb, 2)),
                dma((nb, 2)),
                dma((nb,)),
                dma((nb,)),
                dma((nb, xs // nb * ZS)),
                dma((xs * ZS,)),
            ],
            compiler_params=pltpu.CompilerParams(
                collective_id=0, has_side_effects=True, vmem_limit_bytes=LIMIT
            ),
            name="step_and_render",
        )(*(pltpu.with_memory_space_constraint(v, pltpu.HBM) for v in (fields, conductance, absorption, occupancy, facing)))
        return pl.pallas_call(
            hand_over,
            out_shape=tuple(pltpu.HBM(v.shape, f32) for v in held),
            in_specs=[in_vmem, in_vmem],
            out_specs=(hbm, hbm),
            scratch_shapes=[dma((cx + 1,))],
            name="hand_over",
        )(*(pltpu.with_memory_space_constraint(v, pltpu.VMEM) for v in held))

    return jax.shard_map(
        shards,
        mesh=mesh,
        in_specs=(
            P(None, "bx", None, "bz"),
            P("bx", None, "bz"),
            P("bx", None, "bz"),
            P("bx", None, "bz"),
            P(None, "bz"),
        ),
        out_specs=(P(None, "bx", None, "bz"), P(None, "bx", "bz")),
        check_vma=False,
    )
```

```python
import functools

import jax
import jax.numpy as jnp
from jax import lax
from jax.experimental import pallas as pl
from jax.experimental.pallas import tpu as pltpu
from jax.sharding import PartitionSpec as P

MESH = pl.DeviceIdType.MESH
TY = 16
TZ = 32
ZS = 8
PAD = 8
LIMIT = 30 << 20
SHARE = 0.5 / 7.0
UB = 2
PU, AU, BU = 2, 2, 4
SPLIT = 10
EARLY = 1


def spread(flags):
    column = lax.broadcasted_iota(jnp.int32, (flags.shape[0], 128), 0)
    lane = lax.broadcasted_iota(jnp.int32, (flags.shape[0], 128), 1)
    own = (lane // TZ == column).astype(jnp.float32)
    return lax.dot_general(
        flags.astype(jnp.float32), own, (((0,), (0,)), ((), ())), preferred_element_type=jnp.float32
    )


def kernel(
    n_bx, n_bz, cx, ny,
    fields, cond, absn, occ, facing,
    adv, pic,
    u, k, ab, lo, hi, zs, zl, zr, occ_m, fac_m, pair, give, ready, got, flags,
    word, flag_sem, in_sem, hs_sem, hr_sem, zs_sem, zr_sem, cs_sem, cr_sem, as_sem, ar_sem,
):
    xs = n_bx // (2 * ZS)
    nb = ZS // UB
    groups = UB * xs
    bx = lax.axis_index("bx")
    bz = lax.axis_index("bz")
    core = bx % 2
    z = (bx // 2) % ZS
    x = bx // (2 * ZS)
    has_lo, has_hi = bx > 0, bx < n_bx - 1
    has_l, has_r = bz > 0, bz < n_bz - 1
    lo_id, hi_id = (bx - 1, bz), (bx + 1, bz)
    l_id, r_id = (bx, bz - 1), (bx, bz + 1)
    mate = (bx + 1 - 2 * core, bz)

    def chip_id(dx, dz):
        return ((((x + dx) % xs) * ZS + (z + dz) % ZS) * 2 + core, bz)

    def first_row(i, q):
        return pl.multiple_of(i * (8 * ZS) + q * 8, 8)

    barrier = pltpu.get_barrier_semaphore()
    line = [(0, dz) for dz in (1, ZS - 1, 2, ZS - 2, 3, ZS - 3, 4)] + [(dx, 0) for dx in range(1, xs)]

    def greet(sem, who):
        pl.semaphore_signal(sem, inc=1, device_id=who, device_id_type=MESH)

    for near, who in ((has_lo, lo_id), (has_hi, hi_id), (has_l, l_id), (has_r, r_id)):
        @pl.when(near)
        def _():
            greet(barrier, who)
    for dx, dz in line:
        greet(barrier, chip_id(dx, dz))

    body = pl.ds(PAD, ny)
    loads = [pltpu.make_async_copy(fields.at[a], u.at[a, :, body, :], in_sem.at[a]) for a in range(3)]
    loads.append(pltpu.make_async_copy(cond, k.at[:, body, :], in_sem.at[3]))
    late_load = pltpu.make_async_copy(absn, ab, in_sem.at[4])
    for c in loads:
        c.start()

    lane = lax.broadcasted_iota(jnp.int32, (8, 128), 1)
    first, last = lane == 0, lane == 127
    rim = first | last

    slot = ((lane + 1) % 128) // 2

    def edge(b, right):
        return pltpu.make_async_remote_copy(
            zs.at[b], (zl if right else zr).at[b], zs_sem.at[int(right)],
            zr_sem.at[b, int(right)], device_id=r_id if right else l_id, device_id_type=MESH)

    def pack_batch(b):
        def pack(g, carry):
            for h in range(PU):
                r = g * PU + h
                q, i = b * UB + r // xs, r % xs
                at = pl.ds(first_row(i, q) + PAD, 8)
                parts = []
                for a in range(3):
                    out = jnp.zeros((8, 128), jnp.float32)
                    for p in range(cx):
                        j = 3 * p + a
                        v = u[a, p, at, :]
                        out = jnp.where(slot == j, pltpu.roll(v, 2 * j, 1) if j else v, out)
                    parts.append(out)
                out = jnp.zeros((8, 128), jnp.float32)
                for p in range(cx):
                    out = jnp.where(slot == 32 + 3 * p, pltpu.roll(k[p, at, :], 64 + 6 * p, 1), out)
                out = out + pltpu.roll(out, 2, 1) + pltpu.roll(out, 4, 1)
                zs[b, i, pl.ds(pl.multiple_of(r // xs * 8, 8), 8), :] = (parts[0] + parts[1]) + (parts[2] + out)
            return carry

        lax.fori_loop(0, groups // PU, pack, 0)

    def send_edges(b):
        @pl.when(has_l)
        def _():
            edge(b, False).start()

        @pl.when(has_r)
        def _():
            edge(b, True).start()

    if EARLY:
        for c in loads:
            c.wait()
    for b in range(EARLY):
        pack_batch(b)
    pl.semaphore_wait(
        barrier,
        len(line) + has_lo.astype(jnp.int32) + has_hi.astype(jnp.int32)
        + has_l.astype(jnp.int32) + has_r.astype(jnp.int32),
    )

    def halo(b, up):
        who, p = (hi_id, cx - 1) if up else (lo_id, 0)
        to = lo if up else hi
        d = int(up)
        return (
            pltpu.make_async_remote_copy(
                fields.reshape(3, cx, xs, nb, UB * 8, 128).at[:, p, :, b], to.at[b, 0:3],
                hs_sem.at[d], hr_sem.at[b, d], device_id=who, device_id_type=MESH),
            pltpu.make_async_remote_copy(
                cond.reshape(cx, xs, nb, UB * 8, 128).at[p, :, b], to.at[b, 3],
                hs_sem.at[d], hr_sem.at[b, d], device_id=who, device_id_type=MESH),
        )

    def take(ref, sem):
        pltpu.make_async_copy(ref, ref, sem).wait()

    def each_halo(b, up, act):
        @pl.when(has_hi if up else has_lo)
        def _():
            for c in halo(b, up):
                act(c)

    def send_halo(b, carry):
        each_halo(b, False, lambda c: c.start())
        each_halo(b, True, lambda c: c.start())
        return carry

    lax.fori_loop(0, 1, send_halo, 0)
    for b in range(EARLY):
        send_edges(b)
    lax.fori_loop(1, nb, send_halo, 0)
    for dx, dz in line:
        greet(word, chip_id(dx, dz))

    flag_loads = [
        pltpu.make_async_copy(ref, flags.at[i], flag_sem.at[i]) for i, ref in enumerate((occ, facing))
    ]
    late_load.start()
    for c in flag_loads:
        c.start()
    if not EARLY:
        for c in loads:
            c.wait()

    def pack_rest(b, carry):
        pack_batch(b)
        send_edges(b)
        return carry

    if EARLY < nb:
        lax.fori_loop(EARLY, nb, pack_rest, 0)

    for p in range(cx):
        k[p, 0:PAD, :] = jnp.zeros((PAD, 128), jnp.float32)
        k[p, PAD + ny : 2 * PAD + ny, :] = jnp.zeros((PAD, 128), jnp.float32)
        for a in range(3):
            u[a, p, 0:PAD, :] = jnp.zeros((PAD, 128), jnp.float32)
            u[a, p, PAD + ny : 2 * PAD + ny, :] = jnp.zeros((PAD, 128), jnp.float32)

    @pl.when(bx == 0)
    def _():
        lo[...] = jnp.zeros_like(lo)

    @pl.when(bx == n_bx - 1)
    def _():
        hi[...] = jnp.zeros_like(hi)

    @pl.when(bz == 0)
    def _():
        zl[...] = jnp.zeros_like(zl)

    @pl.when(bz == n_bz - 1)
    def _():
        zr[...] = jnp.zeros_like(zr)

    for c in flag_loads:
        c.wait()
    occ_m[...] = spread(flags[0])
    fac_m[...] = spread(flags[1])

    def interior(n, carry):
        for h in range(AU):
            r = n * AU + h
            y0 = first_row(r // UB % xs, r // groups * UB + r % UB)
            at = pl.ds(y0, 8)
            mid = pl.ds(y0 + PAD, 8)
            above = pl.ds(y0 + PAD + 1, 8)
            below = pl.ds(y0 + PAD - 1, 8)
            k_here = k[0, mid, :]
            u_here = [u[a, 0, mid, :] for a in range(3)]
            flow = [None] * 3
            for p in range(cx):
                k_a = k_here + k[p, above, :]
                k_b = k_here + k[p, below, :]
                k_r = jnp.where(last, 0.0, k_here + pltpu.roll(k_here, 127, 1))
                if p < cx - 1:
                    k_next = k[p + 1, mid, :]
                    u_next = [u[a, p + 1, mid, :] for a in range(3)]
                    k_x = k_here + k_next
                for a in range(3):
                    v = u_here[a]
                    across = k_r * (pltpu.roll(v, 127, 1) - v)
                    change = across - pltpu.roll(across, 1, 1)
                    change = change + k_a * (u[a, p, above, :] - v)
                    change = change + k_b * (u[a, p, below, :] - v)
                    if p > 0:
                        change = change - flow[a]
                    if p < cx - 1:
                        flow[a] = k_x * (u_next[a] - v)
                        change = change + flow[a]
                    adv[a, p, at, :] = v + change * SHARE
                k_here, u_here = k_next, u_next
        return carry

    lax.fori_loop(0, SPLIT, interior, 0)
    late_load.wait()

    def core_copy(b):
        units = pl.ds(b * UB, UB)
        return pltpu.make_async_remote_copy(
            give.at[units], pair.at[core, units], cs_sem, cr_sem.at[b],
            device_id=mate, device_id_type=MESH)

    def send_out(q, dx):
        to_x = (x + dx) % xs
        return pltpu.make_async_remote_copy(
            ready.at[q, to_x], got.at[x * ZS + z], as_sem, ar_sem,
            device_id=((to_x * ZS + q) * 2 + core, bz), device_id_type=MESH)

    def each_out(q, act):
        for dx in (2, 1, 3):
            act(send_out(q, dx))

        @pl.when(q != z)
        def _():
            act(send_out(q, 0))

    def work(b):
        @pl.when(has_lo)
        def _():
            take(lo.at[b], hr_sem.at[b, 1])

        @pl.when(has_hi)
        def _():
            take(hi.at[b], hr_sem.at[b, 0])

        @pl.when(has_l)
        def _():
            edge(b, True).wait_recv()

        @pl.when(has_r)
        def _():
            edge(b, False).wait_recv()

        def step(n, carry):
            for h in range(BU):
                r = n * BU + h
                q, i = b * UB + r // xs, r % xs
                y0 = first_row(i, q)
                at = pl.ds(y0, 8)
                mid = pl.ds(y0 + PAD, 8)
                here = pl.ds(pl.multiple_of(r // xs * 8, 8), 8)
                own = zs[b, i, here, :]
                other = jnp.where(lane % 2 == 1, pltpu.roll(zr[b, i, here, :], 127, 1), pltpu.roll(zl[b, i, here, :], 1, 1))
                into = pltpu.roll(own + other, 64, 1) * (other - own) * SHARE
                tile = y0 // TY
                mask = occ_m[pl.ds(tile, 1), :]
                flip = jnp.broadcast_to(fac_m[pl.ds(tile, 1), :] > 0.5, (8, 128))
                through = jnp.ones((8, 128), jnp.float32)
                colour = [jnp.zeros((8, 128), jnp.float32)] * 3
                for p in range(cx):
                    new = []
                    if p == 0:
                        k_x = (k[0, mid, :] + lo[b, 3, i, here, :]) * SHARE
                    if p == cx - 1:
                        k_x = (k[p, mid, :] + hi[b, 3, i, here, :]) * SHARE
                    for a in range(3):
                        j = 3 * p + a
                        out = adv[a, p, at, :]
                        out = out + jnp.where(rim, pltpu.roll(into, 128 - 2 * j, 1) if j else into, 0.0)
                        if p == 0:
                            out = out + k_x * (lo[b, a, i, here, :] - u[a, p, mid, :])
                        if p == cx - 1:
                            out = out + k_x * (hi[b, a, i, here, :] - u[a, p, mid, :])
                        adv[a, p, at, :] = out
                        new.append(out)
                    passed = jnp.exp(-(ab[p, at, :] * new[0] * mask))
                    glow = (1.0 - passed) * jnp.where(flip, 1.0, through)
                    keep = jnp.where(flip, passed, 1.0)
                    colour = [colour[a] * keep + new[a] * glow for a in range(3)]
                    through = through * passed
                for c, v in enumerate(colour + [through]):
                    top, bottom = v[0:4], v[4:8]
                    pair[core, q, i, c] = jnp.where(core == 0, top, bottom)
                    give[q, i, c] = jnp.where(core == 0, bottom, top)
            return carry

        lax.fori_loop(0, groups // BU, step, 0)
        core_copy(b).start()

    def merge(b):
        core_copy(b).wait_recv()

        def step(r, carry):
            q, i = b * UB + r // xs, r % xs
            flip = jnp.broadcast_to(fac_m[pl.ds(first_row(i, q) // TY, 1), :] > 0.5, (4, 128))
            t0, t1 = pair[0, q, i, 3], pair[1, q, i, 3]
            for c in range(3):
                c0, c1 = pair[0, q, i, c], pair[1, q, i, c]
                ready[q, i, c] = jnp.where(flip, c1 + t1 * c0, c0 + t0 * c1)
            ready[q, i, 3] = t0 * t1
            return carry

        lax.fori_loop(0, groups, step, 0)

        @pl.when(b == 0)
        def _():
            pl.semaphore_wait(word, len(line))

        for v in range(UB):
            each_out(b * UB + v, lambda c: c.start())

    def batch(n, carry):
        @pl.when(n < nb)
        def _():
            work(n)

        @pl.when(n == 0)
        def _():
            lax.fori_loop(SPLIT, ny // (8 * AU), interior, 0)

        @pl.when(n != 1)
        def _():
            merge(jnp.maximum(n - 1, 0))

        return carry

    lax.fori_loop(0, nb + 1, batch, 0)

    @pl.when(has_lo)
    def _():
        take(hi, hs_sem.at[0])

    @pl.when(has_hi)
    def _():
        take(lo, hs_sem.at[1])

    @pl.when(has_l)
    def _():
        take(zs, zs_sem.at[0])

    @pl.when(has_r)
    def _():
        take(zs, zs_sem.at[1])

    take(give, cs_sem)
    others = got.at[pl.ds(0, xs * ZS - 1)]
    take(others, as_sem)

    flip = jnp.broadcast_to(fac_m[pl.ds(bx * 4 // TY, 1), :] > 0.5, (4, 128))
    me = x * ZS + z
    got[pl.ds(me, 1)] = ready[pl.ds(z, 1), x]

    take(others, ar_sem)

    def gather(s, carry):
        colour, through = list(carry[:3]), carry[3]
        for h in range(ZS):
            t = got[s * ZS + h, 3]
            for c in range(3):
                piece = got[s * ZS + h, c]
                colour[c] = jnp.where(flip, piece + t * colour[c], colour[c] + through * piece)
            through = through * t
        return (*colour, through)

    zero = jnp.zeros((4, 128), jnp.float32)
    out = lax.fori_loop(0, xs, gather, (zero, zero, zero, jnp.ones((4, 128), jnp.float32)))
    for c in range(3):
        pic[c] = out[c]
    pic[3] = 1.0 - out[3]


def hand_over(adv, pic, adv_out, pic_out, sem):
    cx = adv.shape[1]
    copies = [pltpu.make_async_copy(adv.at[:, p], adv_out.at[:, p], sem.at[p]) for p in range(cx)]
    copies.append(pltpu.make_async_copy(pic, pic_out, sem.at[cx]))
    for c in copies:
        c.start()
    for c in copies:
        c.wait()


def solution(mesh):
    n_bx, n_bz = mesh.shape["bx"], mesh.shape["bz"]

    def shards(fields, conductance, absorption, occupancy, facing):
        _, cx, ny, nz = fields.shape
        occupancy = occupancy[0].T
        facing = facing.T
        xs, nb = n_bx // (2 * ZS), ZS // UB
        f32 = jnp.float32
        vmem, dma = pltpu.VMEM, pltpu.SemaphoreType.DMA
        hbm = pl.BlockSpec(memory_space=pltpu.HBM)
        in_vmem = pl.BlockSpec(memory_space=pltpu.VMEM)
        operands = (fields, conductance, absorption, occupancy, facing)
        held = pl.pallas_call(
            functools.partial(kernel, n_bx, n_bz, cx, ny),
            out_shape=(
                jax.ShapeDtypeStruct(fields.shape, f32),
                jax.ShapeDtypeStruct((4, ny // n_bx, nz), f32),
            ),
            in_specs=[hbm] * 5,
            out_specs=(in_vmem, in_vmem),
            scratch_shapes=[
                vmem((3, cx, ny + 2 * PAD, nz), f32),
                vmem((cx, ny + 2 * PAD, nz), f32),
                vmem((cx, ny, nz), f32),
                vmem((nb, 4, xs, UB * 8, nz), f32),
                vmem((nb, 4, xs, UB * 8, nz), f32),
                vmem((nb, xs, UB * 8, nz), f32),
                vmem((nb, xs, UB * 8, nz), f32),
                vmem((nb, xs, UB * 8, nz), f32),
                vmem((ny // TY, nz), f32),
                vmem((ny // TY, nz), f32),
                vmem((2, ZS, xs, 4, 4, nz), f32),
                vmem((ZS, xs, 4, 4, nz), f32),
                vmem((ZS, xs, 4, 4, nz), f32),
                vmem((xs * ZS, 4, 4, nz), f32),
                vmem((2,) + facing.shape, jnp.int32),
                pltpu.SemaphoreType.REGULAR,
                dma((2,)),
                dma((5,)),
                dma((2,)),
                dma((nb, 2)),
                dma((2,)),
                dma((nb, 2)),
                dma(()),
                dma((nb,)),
                dma(()),
                dma(()),
            ],
            compiler_params=pltpu.CompilerParams(
                collective_id=0, has_side_effects=True, vmem_limit_bytes=LIMIT
            ),
            name="step_and_render",
        )(*(pltpu.with_memory_space_constraint(v, pltpu.HBM) for v in operands))
        return pl.pallas_call(
            hand_over,
            out_shape=tuple(pltpu.HBM(v.shape, f32) for v in held),
            in_specs=[in_vmem, in_vmem],
            out_specs=(hbm, hbm),
            scratch_shapes=[dma((cx + 1,))],
            name="hand_over",
        )(*(pltpu.with_memory_space_constraint(v, pltpu.VMEM) for v in held))

    return jax.shard_map(
        shards,
        mesh=mesh,
        in_specs=(
            P(None, "bx", None, "bz"),
            P("bx", None, "bz"),
            P("bx", None, "bz"),
            P("bx", None, "bz"),
            P(None, "bz"),
        ),
        out_specs=(P(None, "bx", None, "bz"), P(None, "bx", "bz")),
        check_vma=False,
    )
```

```python
import functools

import jax
import jax.numpy as jnp
from jax import lax
from jax.experimental import pallas as pl
from jax.experimental.pallas import tpu as pltpu
from jax.sharding import PartitionSpec as P

MESH = pl.DeviceIdType.MESH
TY = 16
TZ = 32
ZS = 8
PAD = 8
LIMIT = 30 << 20
SHARE = 0.5 / 7.0
UB = 2
PU, AU, BU = 4, 2, 8
SPLIT = 10
EARLY = 1


def spread(flags):
    column = lax.broadcasted_iota(jnp.int32, (flags.shape[0], 128), 0)
    lane = lax.broadcasted_iota(jnp.int32, (flags.shape[0], 128), 1)
    own = (lane // TZ == column).astype(jnp.float32)
    return lax.dot_general(
        flags.astype(jnp.float32), own, (((0,), (0,)), ((), ())), preferred_element_type=jnp.float32
    )


def kernel(
    n_bx, n_bz, cx, ny,
    fields, cond, absn, occ, facing,
    adv, pic,
    u, k, ab, lo, hi, zs, zl, zr, occ_m, fac_m, pair, give, ready, got, flags,
    word, flag_sem, in_sem, hs_sem, hr_sem, zs_sem, zr_sem, cs_sem, cr_sem, as_sem, ar_sem,
):
    xs = n_bx // (2 * ZS)
    nb = ZS // UB
    groups = UB * xs
    bx = lax.axis_index("bx")
    bz = lax.axis_index("bz")
    core = bx % 2
    z = (bx // 2) % ZS
    x = bx // (2 * ZS)
    has_lo, has_hi = bx > 0, bx < n_bx - 1
    has_l, has_r = bz > 0, bz < n_bz - 1
    lo_id, hi_id = (bx - 1, bz), (bx + 1, bz)
    l_id, r_id = (bx, bz - 1), (bx, bz + 1)
    mate = (bx + 1 - 2 * core, bz)

    def chip_id(dx, dz):
        return ((((x + dx) % xs) * ZS + (z + dz) % ZS) * 2 + core, bz)

    def first_row(i, q):
        return pl.multiple_of(i * (8 * ZS) + q * 8, 8)

    barrier = pltpu.get_barrier_semaphore()
    line = [(0, dz) for dz in (1, ZS - 1, 2, ZS - 2, 3, ZS - 3, 4)] + [(dx, 0) for dx in range(1, xs)]

    def greet(sem, who):
        pl.semaphore_signal(sem, inc=1, device_id=who, device_id_type=MESH)

    for near, who in ((has_lo, lo_id), (has_hi, hi_id), (has_l, l_id), (has_r, r_id)):
        @pl.when(near)
        def _():
            greet(barrier, who)
    for dx, dz in line:
        greet(barrier, chip_id(dx, dz))

    body = pl.ds(PAD, ny)
    loads = [pltpu.make_async_copy(fields.at[a], u.at[a, :, body, :], in_sem.at[a]) for a in range(3)]
    loads.append(pltpu.make_async_copy(cond, k.at[:, body, :], in_sem.at[3]))
    late_load = pltpu.make_async_copy(absn, ab, in_sem.at[4])
    flag_loads = [
        pltpu.make_async_copy(ref, flags.at[i], flag_sem.at[i]) for i, ref in enumerate((occ, facing))
    ]
    for c in flag_loads + loads:
        c.start()

    lane = lax.broadcasted_iota(jnp.int32, (8, 128), 1)
    first, last = lane == 0, lane == 127
    rim = first | last

    slot = ((lane + 1) % 128) // 2

    def edge(b, right):
        return pltpu.make_async_remote_copy(
            zs.at[b], (zl if right else zr).at[b], zs_sem.at[int(right)],
            zr_sem.at[b, int(right)], device_id=r_id if right else l_id, device_id_type=MESH)

    def pack_batch(b):
        def pack(g, carry):
            for h in range(PU):
                r = g * PU + h
                q, i = b * UB + r // xs, r % xs
                at = pl.ds(first_row(i, q) + PAD, 8)
                parts = []
                for a in range(3):
                    out = jnp.zeros((8, 128), jnp.float32)
                    for p in range(cx):
                        j = 3 * p + a
                        v = u[a, p, at, :]
                        out = jnp.where(slot == j, pltpu.roll(v, 2 * j, 1) if j else v, out)
                    parts.append(out)
                out = jnp.zeros((8, 128), jnp.float32)
                for p in range(cx):
                    out = jnp.where(slot == 32 + 3 * p, pltpu.roll(k[p, at, :], 64 + 6 * p, 1), out)
                out = out + pltpu.roll(out, 2, 1) + pltpu.roll(out, 4, 1)
                zs[b, i, pl.ds(pl.multiple_of(r // xs * 8, 8), 8), :] = (parts[0] + parts[1]) + (parts[2] + out)
            return carry

        lax.fori_loop(0, groups // PU, pack, 0)

    def send_edges(b):
        @pl.when(has_l)
        def _():
            edge(b, False).start()

        @pl.when(has_r)
        def _():
            edge(b, True).start()

    for p in range(cx):
        k[p, 0:PAD, :] = jnp.zeros((PAD, 128), jnp.float32)
        k[p, PAD + ny : 2 * PAD + ny, :] = jnp.zeros((PAD, 128), jnp.float32)
        for a in range(3):
            u[a, p, 0:PAD, :] = jnp.zeros((PAD, 128), jnp.float32)
            u[a, p, PAD + ny : 2 * PAD + ny, :] = jnp.zeros((PAD, 128), jnp.float32)

    @pl.when(bx == 0)
    def _():
        lo[...] = jnp.zeros_like(lo)

    @pl.when(bx == n_bx - 1)
    def _():
        hi[...] = jnp.zeros_like(hi)

    @pl.when(bz == 0)
    def _():
        zl[...] = jnp.zeros_like(zl)

    @pl.when(bz == n_bz - 1)
    def _():
        zr[...] = jnp.zeros_like(zr)

    for c in flag_loads:
        c.wait()
    occ_m[...] = spread(flags[0])
    fac_m[...] = spread(flags[1])

    if EARLY:
        for c in loads:
            c.wait()
    for b in range(EARLY):
        pack_batch(b)
    pl.semaphore_wait(
        barrier,
        len(line) + has_lo.astype(jnp.int32) + has_hi.astype(jnp.int32)
        + has_l.astype(jnp.int32) + has_r.astype(jnp.int32),
    )

    def halo(b, up):
        who, p = (hi_id, cx - 1) if up else (lo_id, 0)
        to = lo if up else hi
        d = int(up)
        return (
            pltpu.make_async_remote_copy(
                fields.reshape(3, cx, xs, nb, UB * 8, 128).at[:, p, :, b], to.at[b, 0:3],
                hs_sem.at[d], hr_sem.at[b, d], device_id=who, device_id_type=MESH),
            pltpu.make_async_remote_copy(
                cond.reshape(cx, xs, nb, UB * 8, 128).at[p, :, b], to.at[b, 3],
                hs_sem.at[d], hr_sem.at[b, d], device_id=who, device_id_type=MESH),
        )

    def take(ref, sem):
        pltpu.make_async_copy(ref, ref, sem).wait()

    def each_halo(b, up, act):
        @pl.when(has_hi if up else has_lo)
        def _():
            for c in halo(b, up):
                act(c)

    def send_halo(b, carry):
        each_halo(b, False, lambda c: c.start())
        each_halo(b, True, lambda c: c.start())
        return carry

    lax.fori_loop(0, 1, send_halo, 0)
    for b in range(EARLY):
        send_edges(b)
    lax.fori_loop(1, nb, send_halo, 0)
    for dx, dz in line:
        greet(word, chip_id(dx, dz))

    late_load.start()
    if not EARLY:
        for c in loads:
            c.wait()

    def pack_rest(b, carry):
        pack_batch(b)
        send_edges(b)
        return carry

    if EARLY < nb:
        lax.fori_loop(EARLY, nb, pack_rest, 0)

    def interior(n, carry):
        for h in range(AU):
            r = n * AU + h
            y0 = first_row(r // UB % xs, r // groups * UB + r % UB)
            at = pl.ds(y0, 8)
            mid = pl.ds(y0 + PAD, 8)
            above = pl.ds(y0 + PAD + 1, 8)
            below = pl.ds(y0 + PAD - 1, 8)
            k_here = k[0, mid, :]
            u_here = [u[a, 0, mid, :] for a in range(3)]
            flow = [None] * 3
            for p in range(cx):
                k_a = k_here + k[p, above, :]
                k_b = k_here + k[p, below, :]
                k_r = jnp.where(last, 0.0, k_here + pltpu.roll(k_here, 127, 1))
                if p < cx - 1:
                    k_next = k[p + 1, mid, :]
                    u_next = [u[a, p + 1, mid, :] for a in range(3)]
                    k_x = k_here + k_next
                for a in range(3):
                    v = u_here[a]
                    across = k_r * (pltpu.roll(v, 127, 1) - v)
                    change = across - pltpu.roll(across, 1, 1)
                    change = change + k_a * (u[a, p, above, :] - v)
                    change = change + k_b * (u[a, p, below, :] - v)
                    if p > 0:
                        change = change - flow[a]
                    if p < cx - 1:
                        flow[a] = k_x * (u_next[a] - v)
                        change = change + flow[a]
                    adv[a, p, at, :] = v + change * SHARE
                k_here, u_here = k_next, u_next
        return carry

    lax.fori_loop(0, SPLIT, interior, 0)
    late_load.wait()

    def core_copy(b):
        units = pl.ds(b * UB, UB)
        return pltpu.make_async_remote_copy(
            give.at[units], pair.at[core, units], cs_sem, cr_sem.at[b],
            device_id=mate, device_id_type=MESH)

    def send_out(q, dx):
        to_x = (x + dx) % xs
        return pltpu.make_async_remote_copy(
            ready.at[q, to_x], got.at[x * ZS + z], as_sem, ar_sem,
            device_id=((to_x * ZS + q) * 2 + core, bz), device_id_type=MESH)

    def each_out(q, act):
        for dx in (2, 1, 3):
            act(send_out(q, dx))

        @pl.when(q != z)
        def _():
            act(send_out(q, 0))

    def work(b):
        @pl.when(has_lo)
        def _():
            take(lo.at[b], hr_sem.at[b, 1])

        @pl.when(has_hi)
        def _():
            take(hi.at[b], hr_sem.at[b, 0])

        @pl.when(has_l)
        def _():
            edge(b, True).wait_recv()

        @pl.when(has_r)
        def _():
            edge(b, False).wait_recv()

        def step(n, carry):
            for h in range(BU):
                r = n * BU + h
                q, i = b * UB + r // xs, r % xs
                y0 = first_row(i, q)
                at = pl.ds(y0, 8)
                mid = pl.ds(y0 + PAD, 8)
                here = pl.ds(pl.multiple_of(r // xs * 8, 8), 8)
                own = zs[b, i, here, :]
                other = jnp.where(lane % 2 == 1, pltpu.roll(zr[b, i, here, :], 127, 1), pltpu.roll(zl[b, i, here, :], 1, 1))
                into = pltpu.roll(own + other, 64, 1) * (other - own) * SHARE
                tile = y0 // TY
                mask = occ_m[pl.ds(tile, 1), :]
                flip = jnp.broadcast_to(fac_m[pl.ds(tile, 1), :] > 0.5, (8, 128))
                through = jnp.ones((8, 128), jnp.float32)
                colour = [jnp.zeros((8, 128), jnp.float32)] * 3
                for p in range(cx):
                    new = []
                    if p == 0:
                        k_x = (k[0, mid, :] + lo[b, 3, i, here, :]) * SHARE
                    if p == cx - 1:
                        k_x = (k[p, mid, :] + hi[b, 3, i, here, :]) * SHARE
                    for a in range(3):
                        j = 3 * p + a
                        out = adv[a, p, at, :]
                        out = out + jnp.where(rim, pltpu.roll(into, 128 - 2 * j, 1) if j else into, 0.0)
                        if p == 0:
                            out = out + k_x * (lo[b, a, i, here, :] - u[a, p, mid, :])
                        if p == cx - 1:
                            out = out + k_x * (hi[b, a, i, here, :] - u[a, p, mid, :])
                        adv[a, p, at, :] = out
                        new.append(out)
                    passed = jnp.exp(-(ab[p, at, :] * new[0] * mask))
                    glow = (1.0 - passed) * jnp.where(flip, 1.0, through)
                    keep = jnp.where(flip, passed, 1.0)
                    colour = [colour[a] * keep + new[a] * glow for a in range(3)]
                    through = through * passed
                for c, v in enumerate(colour + [through]):
                    top, bottom = v[0:4], v[4:8]
                    pair[core, q, i, c] = jnp.where(core == 0, top, bottom)
                    give[q, i, c] = jnp.where(core == 0, bottom, top)
            return carry

        lax.fori_loop(0, groups // BU, step, 0)
        core_copy(b).start()

    def merge(b):
        core_copy(b).wait_recv()

        def step(v, carry):
            q = b * UB + v
            for i in range(xs):
                flip = jnp.broadcast_to(fac_m[pl.ds(first_row(i, q) // TY, 1), :] > 0.5, (4, 128))
                t0, t1 = pair[0, q, i, 3], pair[1, q, i, 3]
                for c in range(3):
                    c0, c1 = pair[0, q, i, c], pair[1, q, i, c]
                    ready[q, i, c] = jnp.where(flip, c1 + t1 * c0, c0 + t0 * c1)
                ready[q, i, 3] = t0 * t1
            return carry

        lax.fori_loop(0, UB, step, 0)

        @pl.when(b == 0)
        def _():
            pl.semaphore_wait(word, len(line))

        for v in range(UB):
            each_out(b * UB + v, lambda c: c.start())

    def batch(n, carry):
        @pl.when(n < nb)
        def _():
            work(n)

        @pl.when(n == 0)
        def _():
            lax.fori_loop(SPLIT, ny // (8 * AU), interior, 0)

        @pl.when(n != 1)
        def _():
            merge(jnp.maximum(n - 1, 0))

        return carry

    lax.fori_loop(0, nb + 1, batch, 0)

    @pl.when(has_lo)
    def _():
        take(hi, hs_sem.at[0])

    @pl.when(has_hi)
    def _():
        take(lo, hs_sem.at[1])

    @pl.when(has_l)
    def _():
        take(zs, zs_sem.at[0])

    @pl.when(has_r)
    def _():
        take(zs, zs_sem.at[1])

    take(give, cs_sem)
    others = got.at[pl.ds(0, xs * ZS - 1)]
    take(others, as_sem)

    flip = jnp.broadcast_to(fac_m[pl.ds(bx * 4 // TY, 1), :] > 0.5, (4, 128))
    me = x * ZS + z
    got[pl.ds(me, 1)] = ready[pl.ds(z, 1), x]

    take(others, ar_sem)

    def gather(s, carry):
        colour, through = list(carry[:3]), carry[3]
        for h in range(ZS):
            t = got[s * ZS + h, 3]
            for c in range(3):
                piece = got[s * ZS + h, c]
                colour[c] = jnp.where(flip, piece + t * colour[c], colour[c] + through * piece)
            through = through * t
        return (*colour, through)

    zero = jnp.zeros((4, 128), jnp.float32)
    out = lax.fori_loop(0, xs, gather, (zero, zero, zero, jnp.ones((4, 128), jnp.float32)))
    for c in range(3):
        pic[c] = out[c]
    pic[3] = 1.0 - out[3]


def hand_over(adv, pic, adv_out, pic_out, sem):
    cx = adv.shape[1]
    copies = [pltpu.make_async_copy(adv.at[:, p], adv_out.at[:, p], sem.at[p]) for p in range(cx)]
    copies.append(pltpu.make_async_copy(pic, pic_out, sem.at[cx]))
    for c in copies:
        c.start()
    for c in copies:
        c.wait()


def solution(mesh):
    n_bx, n_bz = mesh.shape["bx"], mesh.shape["bz"]

    def shards(fields, conductance, absorption, occupancy, facing):
        _, cx, ny, nz = fields.shape
        occupancy = occupancy[0].T
        facing = facing.T
        xs, nb = n_bx // (2 * ZS), ZS // UB
        f32 = jnp.float32
        vmem, dma = pltpu.VMEM, pltpu.SemaphoreType.DMA
        hbm = pl.BlockSpec(memory_space=pltpu.HBM)
        in_vmem = pl.BlockSpec(memory_space=pltpu.VMEM)
        operands = (fields, conductance, absorption, occupancy, facing)
        held = pl.pallas_call(
            functools.partial(kernel, n_bx, n_bz, cx, ny),
            out_shape=(
                jax.ShapeDtypeStruct(fields.shape, f32),
                jax.ShapeDtypeStruct((4, ny // n_bx, nz), f32),
            ),
            in_specs=[hbm] * 5,
            out_specs=(in_vmem, in_vmem),
            scratch_shapes=[
                vmem((3, cx, ny + 2 * PAD, nz), f32),
                vmem((cx, ny + 2 * PAD, nz), f32),
                vmem((cx, ny, nz), f32),
                vmem((nb, 4, xs, UB * 8, nz), f32),
                vmem((nb, 4, xs, UB * 8, nz), f32),
                vmem((nb, xs, UB * 8, nz), f32),
                vmem((nb, xs, UB * 8, nz), f32),
                vmem((nb, xs, UB * 8, nz), f32),
                vmem((ny // TY, nz), f32),
                vmem((ny // TY, nz), f32),
                vmem((2, ZS, xs, 4, 4, nz), f32),
                vmem((ZS, xs, 4, 4, nz), f32),
                vmem((ZS, xs, 4, 4, nz), f32),
                vmem((xs * ZS, 4, 4, nz), f32),
                vmem((2,) + facing.shape, jnp.int32),
                pltpu.SemaphoreType.REGULAR,
                dma((2,)),
                dma((5,)),
                dma((2,)),
                dma((nb, 2)),
                dma((2,)),
                dma((nb, 2)),
                dma(()),
                dma((nb,)),
                dma(()),
                dma(()),
            ],
            compiler_params=pltpu.CompilerParams(
                collective_id=0, has_side_effects=True, vmem_limit_bytes=LIMIT
            ),
            name="step_and_render",
        )(*(pltpu.with_memory_space_constraint(v, pltpu.HBM) for v in operands))
        return pl.pallas_call(
            hand_over,
            out_shape=tuple(pltpu.HBM(v.shape, f32) for v in held),
            in_specs=[in_vmem, in_vmem],
            out_specs=(hbm, hbm),
            scratch_shapes=[dma((cx + 1,))],
            name="hand_over",
        )(*(pltpu.with_memory_space_constraint(v, pltpu.VMEM) for v in held))

    return jax.shard_map(
        shards,
        mesh=mesh,
        in_specs=(
            P(None, "bx", None, "bz"),
            P("bx", None, "bz"),
            P("bx", None, "bz"),
            P("bx", None, "bz"),
            P(None, "bz"),
        ),
        out_specs=(P(None, "bx", None, "bz"), P(None, "bx", "bz")),
        check_vma=False,
    )
```
